512 devices in a mesh: gx: 32 (over z, y_hi), gy: 16 (over y_lo, x, core).
Axes of the slice: x: 4, y: 8 (y_hi: 4, y_lo: 2; y = y_hi * 2 + y_lo), z: 8, core: 2. Of those that a mesh axis runs over, the one named last changes fastest.
Arguments:
- random_vectors: float32 [2, 256, 1024, 128], P(None, 'gx', 'gy'), may hold values from -6 to 6
- disorder: float32 [256, 1024, 128], P('gx', 'gy'), may hold values from -2 to 4
Outputs:
- moments: float32 [2, 10], replicated
- last_vectors: float32 [2, 256, 1024, 128], P(None, 'gx', 'gy')
The draws below stay inside these ranges and needn't reach their ends.
All inputs are finite; a program needn't handle non-finite values.
Results may differ from the reference program's by a relative error of at most 0.0001.
Values sent between devices are 32-bit elements; how exact they have to be, the bound alone decides.
A program may use at most 64 MiB of HBM per device.

```python
import jax
import jax.numpy as jnp
from jax import lax

NZ = 128
ITERS = 9
NX = 256
NY = 1024


def block_levels(rng, dims, cuts, low, largest):
    level = 1.0
    for position, parts in cuts:
        draws = jax.random.uniform(jax.random.fold_in(jax.random.fold_in(rng, 6), position), (parts,), jnp.float32, low / len(cuts), largest / len(cuts))
        level = level * jnp.repeat(jnp.exp(draws), dims[position] // parts).reshape((-1,) + (1,) * (len(dims) - 1 - position))
    return level


def noise(stream_key, extent, deviation, reach, split=(), dtype=jnp.bfloat16):
    values = jax.random.normal(stream_key, extent, jnp.float32) * deviation
    if len(split) > 0:
        values = block_levels(stream_key, extent, split, -0.22, 0.18) * values
    return jnp.clip(values, min=-reach, max=reach).astype(dtype)


def setup_inputs(seed: int = 0) -> dict:
    key_of = jax.random.split(jax.random.key(seed), 3)
    random_vectors = noise(key_of[0], (2, NX, NY, NZ), 1.0, 6.0, ((1, 32), (2, 16)), jnp.float32)
    disorder = jnp.clip(-2.0 + 6.0 * jax.random.uniform(key_of[1], (NX, NY, NZ), jnp.float32) ** block_levels(key_of[1], (NX, NY, NZ), ((0, 32), (1, 16)), -0.2, 0.2), -2.0, 4.0)
    return dict(random_vectors=random_vectors, disorder=disorder)


energy_scale = 10.5


def hamilton(field, disorder):
    beside = jnp.roll(field, -1, 0) + jnp.roll(field, 1, 0)
    beside = beside + jnp.roll(field, -1, 1) + jnp.roll(field, 1, 1)
    beside = beside + jnp.roll(field, -1, 2) + jnp.roll(field, 1, 2)
    return (disorder * field - beside) / energy_scale


def one_vector(start, disorder):
    moments_list = [jnp.sum(start * start)]
    previous = start
    current = hamilton(start, disorder)
    moments_list.append(jnp.sum(start * current))
    for step in range(ITERS - 1):
        following = 2.0 * hamilton(current, disorder) - previous
        previous, current = current, following
        moments_list.append(jnp.sum(start * current))
    return jnp.stack(moments_list), current


def reference(random_vectors, disorder):
    sites = NX * NY * NZ
    moments, last_vectors = lax.map(lambda start: one_vector(start, disorder), random_vectors)
    return moments / jnp.float32(sites), last_vectors
```

```python
import functools

import jax
import jax.numpy as jnp
from jax import lax
from jax.experimental import pallas as pl
from jax.experimental.pallas import tpu as pltpu
from jax.sharding import PartitionSpec as P

MESH = pl.DeviceIdType.MESH
ITERS = 9
ENERGY_SCALE = 10.5
TILE = 8
HALO = 3
ROW0 = 2 * TILE
WIDTHS = (3, 2, 2, 2)
SIDES = ((-1, 0), (1, 0), (0, -1), (0, 1), (-1, -1), (-1, 1), (1, -1), (1, 1))
X_SIDES = (0, 1, 4, 5, 6, 7)
Y_SIDES = (2, 3)
GROUP = 8


def body(start_ref, disorder_ref, moments_ref, last_ref, v, energy, sums, partial, local_sem, send_sem, recv_sem, sum_send, sum_recv):
    _, nx, ny, nz = start_ref.shape
    sx, sy = lax.axis_size("gx"), lax.axis_size("gy")
    gx, gy = lax.axis_index("gx"), lax.axis_index("gy")
    x_first, x_end = HALO, HALO + nx
    y_end = ROW0 + ny
    sites = nx * ny * nz * sx * sy

    def beside(dx, dy):
        return (lax.rem(gx + sx + dx, sx), lax.rem(gy + sy + dy, sy))

    z, y_hi = gx // 4, gx % 4
    y_lo, xc = gy // GROUP, gy % GROUP
    y = y_hi * 2 + y_lo
    places = (xc, y, z)

    def partner(turn, d):
        if turn == 0:
            return (gx, y_lo * GROUP + (xc + d) % GROUP)
        if turn == 1:
            to = (y + d) % GROUP
            return (z * 4 + to // 2, (to % 2) * GROUP + xc)
        return (((z + d) % GROUP) * 4 + y_hi, gy)

    barrier = pltpu.get_barrier_semaphore()
    for dx, dy in SIDES:
        pl.semaphore_signal(barrier, inc=1, device_id=beside(dx, dy), device_id_type=MESH)
    for turn in range(3):
        for d in range(1, GROUP):
            pl.semaphore_signal(barrier, inc=1, device_id=partner(turn, d), device_id_type=MESH)

    own = [pltpu.make_async_copy(start_ref.at[k], v.at[k, 0, pl.ds(x_first, nx), pl.ds(ROW0, ny)], local_sem.at[k]) for k in range(2)]
    own.append(pltpu.make_async_copy(disorder_ref, energy.at[pl.ds(x_first, nx), pl.ds(ROW0, ny)], local_sem.at[2]))
    for copy in own:
        copy.start()
    pl.semaphore_wait(barrier, len(SIDES) + 3 * (GROUP - 1))

    buffers = (0, 2, 1, 2)

    def message(e, k, side):
        dx, dy = SIDES[side]
        width = WIDTHS[e] - (k == 2) - (dx != 0 and dy != 0)
        x_from, x_size, x_to = {
            -1: (0, width, x_end),
            0: (0, nx, x_first),
            1: (nx - width, width, x_first - width),
        }[dx]
        y_from, y_size, y_to = {
            -1: (0, TILE, y_end),
            0: (0, ny, ROW0),
            1: (ny - TILE, TILE, ROW0 - TILE),
        }[dy]
        here = (pl.ds(x_from, x_size), pl.ds(y_from, y_size))
        there = (pl.ds(x_to, x_size), pl.ds(y_to, y_size))
        if k == 2:
            src, dst = disorder_ref.at[here], energy.at[there]
        else:
            b = buffers[e]
            if e == 0:
                src = start_ref.at[(k, *here)]
            else:
                src = v.at[k, b, pl.ds(x_first + x_from, x_size), pl.ds(ROW0 + y_from, y_size)]
            dst = v.at[(k, b, *there)]
        return pltpu.make_async_remote_copy(
            src_ref=src,
            dst_ref=dst,
            send_sem=send_sem.at[e, k, side],
            recv_sem=recv_sem.at[e, k, side],
            device_id=beside(dx, dy),
            device_id_type=MESH,
        )

    def send(e, k):
        for side in range(len(SIDES)):
            message(e, k, side).start()

    def arrived(e, k, sides):
        for side in sides:
            message(e, k, side).wait_recv()

    def sent(e, k):
        for side in range(len(SIDES)):
            message(e, k, side).wait_send()

    def advance(k, now, before, after, x0, x1, wide, moment=None):
        r0, r1 = (ROW0 - TILE, y_end + TILE) if wide else (ROW0, y_end)
        factor = (1.0 if before is None else 2.0) / ENERGY_SCALE

        def layer(x, totals):
            for r in range(r0, r1, TILE):
                rows = pl.ds(r, TILE)
                center = v[k, now, x, rows, :]
                total = v[k, now, x + 1, rows, :] + v[k, now, x - 1, rows, :]
                total = total + v[k, now, x, pl.ds(r + 1, TILE), :] + v[k, now, x, pl.ds(r - 1, TILE), :]
                total = total + pltpu.roll(center, nz - 1, 1) + pltpu.roll(center, 1, 1)
                result = (energy[x, rows, :] * center - total) * factor
                if before is not None:
                    result = result - v[k, before, x, rows, :]
                v[k, after, x, rows, :] = result
                if moment is not None and ROW0 <= r < y_end:
                    totals = (totals[0] + center * center, totals[1] + center * result)
            return totals

        zero = jnp.zeros((TILE, nz), jnp.float32)
        totals = lax.fori_loop(x0, x1, layer, (zero, zero))
        if moment is not None:
            for i in range(2):
                sums[k, 2 * moment + i] += totals[i]

    sums[...] = jnp.zeros_like(sums)
    send(0, 0)
    send(0, 2)
    send(0, 1)

    for k in range(2):
        own[k].wait()
        arrived(0, k, range(len(SIDES)))
        if k == 0:
            own[2].wait()
            arrived(0, 2, range(len(SIDES)))
        advance(k, 0, None, 1, x_first - 2, x_first, True)
        advance(k, 0, None, 1, x_first, x_end, True, 0)
        advance(k, 0, None, 1, x_end, x_end + 2, True)
        advance(k, 1, 0, 0, x_first - 1, x_first, True)
        advance(k, 1, 0, 0, x_first, x_end, True, 1)
        advance(k, 1, 0, 0, x_end, x_end + 1, True)
        advance(k, 0, 1, 2, x_first, x_end, False, 2)
        send(1, k)

    def sum_message(turn, d):
        return pltpu.make_async_remote_copy(
            src_ref=partial.at[turn, places[turn]],
            dst_ref=partial.at[turn, places[turn]],
            send_sem=sum_send.at[turn, d],
            recv_sem=sum_recv.at[turn, d],
            device_id=partner(turn, d),
            device_id_type=MESH,
        )

    def sum_arrival(turn, d):
        place = (places[turn] + GROUP - d) % GROUP
        return pltpu.make_async_remote_copy(
            src_ref=partial.at[turn, place],
            dst_ref=partial.at[turn, place],
            send_sem=sum_send.at[turn, d],
            recv_sem=sum_recv.at[turn, d],
            device_id=partner(turn, d),
            device_id_type=MESH,
        )

    def sum_start(turn, row):
        partial[turn, places[turn]] = row
        for d in range(1, GROUP):
            sum_message(turn, d).start()

    def sum_finish(turn):
        for d in range(1, GROUP):
            sum_arrival(turn, d).wait_recv()
        row = partial[turn, 0]
        for place in range(1, GROUP):
            row = row + partial[turn, place]
        return row

    def own_moments():
        lanes = lax.broadcasted_iota(jnp.int32, (1, nz), 1)
        row = jnp.zeros((1, nz), jnp.float32)
        for k in range(2):
            for i in range(ITERS + 1):
                total = sums[k, i]
                if i >= 2:
                    total = 2.0 * total - sums[k, i % 2]
                total = jnp.sum(total, axis=0, keepdims=True)
                total = jnp.sum(total, axis=1, keepdims=True) / jnp.float32(sites)
                row = row + jnp.where(lanes == k * (nz // 2) + i, total, 0.0)
        return row

    for e in range(1, len(WIDTHS)):
        now, after = buffers[e], (1, 2, 1)[e - 1]
        moment = 3 if e == 1 else None
        later = 4 if e == 1 else None
        for k in range(2):
            arrived(e, k, Y_SIDES)
            advance(k, now, 0, 0, x_first + 1, x_end - 1, True, moment)
            if e >= 2:
                sent(e - 1, k)
            advance(k, 0, now, after, x_first + 2, x_end - 2, False, later)
        if e == 3:
            sum_start(2, sum_finish(1))
        for k in range(2):
            arrived(e, k, X_SIDES)
            advance(k, now, 0, 0, x_first - 1, x_first, True)
            advance(k, now, 0, 0, x_first, x_first + 1, True, moment)
            advance(k, 0, now, after, x_first, x_first + 2, False, later)
            advance(k, now, 0, 0, x_end - 1, x_end, True, moment)
            advance(k, now, 0, 0, x_end, x_end + 1, True)
            advance(k, 0, now, after, x_end - 2, x_end, False, later)
            if e + 1 < len(WIDTHS):
                send(e + 1, k)
            else:
                pltpu.make_async_copy(v.at[k, after, pl.ds(x_first, nx), pl.ds(ROW0, ny)], last_ref.at[k], local_sem.at[k]).start()
            if e == 2 and k == 0:
                sum_start(1, sum_finish(0))
        if e == 1:
            sum_start(0, own_moments())

    row = sum_finish(2)
    moments_ref[0:1, :] = row[:, : ITERS + 1]
    moments_ref[1:2, :] = pltpu.roll(row, nz // 2, 1)[:, : ITERS + 1]
    for k in range(3):
        sent(0, k)
    for k in range(2):
        sent(3, k)
    for turn in range(3):
        for d in range(1, GROUP):
            sum_message(turn, d).wait_send()
    for k in range(2):
        pltpu.make_async_copy(v.at[k, 1, pl.ds(x_first, nx), pl.ds(ROW0, ny)], last_ref.at[k], local_sem.at[k]).wait()


def local(random_vectors, disorder):
    vectors, nx, ny, nz = random_vectors.shape
    padded = (nx + 2 * HALO, ny + 2 * ROW0, nz)
    exchanges = (len(WIDTHS), vectors + 1, len(SIDES))
    return pl.pallas_call(
        body,
        out_shape=(
            jax.ShapeDtypeStruct((vectors, ITERS + 1), jnp.float32),
            jax.ShapeDtypeStruct(random_vectors.shape, jnp.float32),
        ),
        in_specs=[pl.BlockSpec(memory_space=pl.ANY)] * 2,
        out_specs=(pl.BlockSpec(memory_space=pltpu.VMEM), pl.BlockSpec(memory_space=pl.ANY)),
        scratch_shapes=[
            pltpu.VMEM((vectors, 3, *padded), jnp.float32),
            pltpu.VMEM(padded, jnp.float32),
            pltpu.VMEM((vectors, ITERS + 1, TILE, nz), jnp.float32),
            pltpu.VMEM((3, GROUP, 1, nz), jnp.float32),
            pltpu.SemaphoreType.DMA((3,)),
            pltpu.SemaphoreType.DMA(exchanges),
            pltpu.SemaphoreType.DMA(exchanges),
            pltpu.SemaphoreType.DMA((3, GROUP)),
            pltpu.SemaphoreType.DMA((3, GROUP)),
        ],
        compiler_params=pltpu.CompilerParams(collective_id=0, has_side_effects=True, vmem_limit_bytes=48 * 2**20),
    )(random_vectors, disorder)


def solution(mesh):
    placed = (P(None, "gx", "gy", None), P("gx", "gy", None))
    return jax.shard_map(
        local,
        mesh=mesh,
        in_specs=placed,
        out_specs=(P(), P(None, "gx", "gy", None)),
        check_vma=False,
    )
```

```python
import functools

import jax
import jax.numpy as jnp
from jax import lax
from jax.experimental import pallas as pl
from jax.experimental.pallas import tpu as pltpu
from jax.sharding import PartitionSpec as P

MESH = pl.DeviceIdType.MESH
ITERS = 9
ENERGY_SCALE = 10.5
TILE = 8
HALO = 3
ROW0 = 2 * TILE
PARITIES = 2
WIDTHS = (3, 2, 2, 2)
SIDES = ((-1, 0), (1, 0), (0, -1), (0, 1), (-1, -1), (-1, 1), (1, -1), (1, 1))
X_SIDES = (0, 1, 4, 5, 6, 7)
Y_SIDES = (2, 3)
GROUP = 8


def body(start_ref, disorder_ref, moments_ref, last_ref, v, energy, sums, partial, local_sem, send_sem, recv_sem, sum_send, sum_recv):
    _, nx, ny, nz = start_ref.shape
    sx, sy = lax.axis_size("gx"), lax.axis_size("gy")
    gx, gy = lax.axis_index("gx"), lax.axis_index("gy")
    x_first, x_end = HALO, HALO + nx
    y_end = ROW0 + ny
    sites = nx * ny * nz * sx * sy

    def beside(dx, dy):
        return (lax.rem(gx + sx + dx, sx), lax.rem(gy + sy + dy, sy))

    z, y_hi = gx // 4, gx % 4
    y_lo, xc = gy // GROUP, gy % GROUP
    y = y_hi * 2 + y_lo
    places = (xc, y, z)

    def partner(turn, d):
        if turn == 0:
            return (gx, y_lo * GROUP + (xc + d) % GROUP)
        if turn == 1:
            to = (y + d) % GROUP
            return (z * 4 + to // 2, (to % 2) * GROUP + xc)
        return (((z + d) % GROUP) * 4 + y_hi, gy)

    barrier = pltpu.get_barrier_semaphore()
    for dx, dy in reversed(SIDES):
        pl.semaphore_signal(barrier, inc=1, device_id=beside(dx, dy), device_id_type=MESH)
    for turn in reversed(range(3)):
        for d in range(1, GROUP):
            pl.semaphore_signal(barrier, inc=1, device_id=partner(turn, d), device_id_type=MESH)

    own = [pltpu.make_async_copy(start_ref.at[k], v.at[k, 0, pl.ds(x_first, nx), pl.ds(ROW0, ny)], local_sem.at[k]) for k in range(2)]
    own.append(pltpu.make_async_copy(disorder_ref, energy.at[pl.ds(x_first, nx), pl.ds(ROW0, ny)], local_sem.at[2]))
    for copy in own:
        copy.start()
    pl.semaphore_wait(barrier, len(SIDES) + 3 * (GROUP - 1))

    buffers = (0, 2, 1, 2)

    def message(e, k, side):
        dx, dy = SIDES[side]
        width = WIDTHS[e] - (k == 2) - (dx != 0 and dy != 0)
        x_from, x_size, x_to = {
            -1: (0, width, x_end),
            0: (0, nx, x_first),
            1: (nx - width, width, x_first - width),
        }[dx]
        y_from, y_size, y_to = {
            -1: (0, width, y_end),
            0: (0, ny, ROW0),
            1: (ny - width, width, ROW0 - width),
        }[dy]
        here = (pl.ds(x_from, x_size), pl.ds(y_from, y_size))
        there = (pl.ds(x_to, x_size), pl.ds(y_to, y_size))
        if k == 2:
            src, dst = disorder_ref.at[here], energy.at[there]
        else:
            b = buffers[e]
            if e == 0:
                src = start_ref.at[(k, *here)]
            else:
                src = v.at[k, b, pl.ds(x_first + x_from, x_size), pl.ds(ROW0 + y_from, y_size)]
            dst = v.at[(k, b, *there)]
        return pltpu.make_async_remote_copy(
            src_ref=src,
            dst_ref=dst,
            send_sem=send_sem.at[e % PARITIES, k],
            recv_sem=recv_sem.at[e % PARITIES, k, int(side in X_SIDES)],
            device_id=beside(dx, dy),
            device_id_type=MESH,
        )

    def send(e, k):
        for side in range(len(SIDES)):
            message(e, k, side).start()

    def rows_of(e, k, sides):
        total = 0
        for side in sides:
            dx, dy = SIDES[side]
            width = WIDTHS[e] - (k == 2) - (dx != 0 and dy != 0)
            total += (width if dx else nx) * (width if dy else ny)
        return total

    def wait_for(rows, semaphore):
        planes = next(n for n in range(1, v.shape[2]) if rows % n == 0 and rows // n <= v.shape[3])
        whole = v.at[0, 0, pl.ds(0, planes), pl.ds(0, rows // planes)]
        pltpu.make_async_copy(whole, whole, semaphore).wait()

    def arrived(e, k, sides):
        wait_for(rows_of(e, k, sides), recv_sem.at[e % PARITIES, k, int(sides == X_SIDES)])

    def sent(e, k):
        wait_for(rows_of(e, k, range(len(SIDES))), send_sem.at[e % PARITIES, k])

    def advance(k, now, before, after, x0, x1, wide, moment=None):
        r0, r1 = (ROW0 - TILE, y_end + TILE) if wide else (ROW0, y_end)
        factor = (1.0 if before is None else 2.0) / ENERGY_SCALE
        layers, rows = pl.ds(x0, x1 - x0), pl.ds(r0, r1 - r0)
        center = v[k, now, layers, rows, :]
        total = v[k, now, pl.ds(x0 + 1, x1 - x0), rows, :] + v[k, now, pl.ds(x0 - 1, x1 - x0), rows, :]
        total = total + v[k, now, layers, pl.ds(r0 + 1, r1 - r0), :] + v[k, now, layers, pl.ds(r0 - 1, r1 - r0), :]
        total = total + pltpu.roll(center, nz - 1, 2) + pltpu.roll(center, 1, 2)
        result = (energy[layers, rows, :] * center - total) * factor
        if before is not None:
            result = result - v[k, before, layers, rows, :]
        if after is None:
            last_ref[k, pl.ds(x0 - x_first, x1 - x0)] = result
        else:
            v[k, after, layers, rows, :] = result
        if moment is not None:
            if wide:
                center, result = center[:, TILE:-TILE], result[:, TILE:-TILE]
            for i, product in enumerate((center * center, center * result)):
                sums[k, 2 * moment + i] += jnp.sum(product.reshape(-1, TILE, nz), axis=0)

    sums[...] = jnp.zeros_like(sums)
    send(0, 2)
    send(0, 0)
    send(0, 1)

    for k in range(2):
        own[k].wait()
        if k == 0:
            own[2].wait()
            arrived(0, 2, Y_SIDES)
            arrived(0, 2, X_SIDES)
        arrived(0, k, Y_SIDES)
        arrived(0, k, X_SIDES)
        advance(k, 0, None, 1, x_first - 2, x_first, True)
        advance(k, 0, None, 1, x_first, x_end, True, 0)
        advance(k, 0, None, 1, x_end, x_end + 2, True)
        advance(k, 1, 0, 0, x_first - 1, x_first, True)
        advance(k, 1, 0, 0, x_first, x_end, True, 1)
        advance(k, 1, 0, 0, x_end, x_end + 1, True)
        advance(k, 0, 1, 2, x_first, x_end, False, 2)
        send(1, k)

    def sum_message(turn, d):
        return pltpu.make_async_remote_copy(
            src_ref=partial.at[turn, places[turn]],
            dst_ref=partial.at[turn, places[turn]],
            send_sem=sum_send.at[turn],
            recv_sem=sum_recv.at[turn],
            device_id=partner(turn, d),
            device_id_type=MESH,
        )

    def sum_start(turn, row):
        partial[turn, places[turn]] = row
        for d in range(1, GROUP):
            sum_message(turn, d).start()

    def sum_finish(turn):
        others = partial.at[turn, pl.ds(0, GROUP - 1)]
        pltpu.make_async_copy(others, others, sum_recv.at[turn]).wait()
        row = partial[turn, 0]
        for place in range(1, GROUP):
            row = row + partial[turn, place]
        return row

    def own_moments():
        lanes = lax.broadcasted_iota(jnp.int32, (1, nz), 1)
        row = jnp.zeros((1, nz), jnp.float32)
        for k in range(2):
            for i in range(ITERS + 1):
                total = sums[k, i]
                if i >= 2:
                    total = 2.0 * total - sums[k, i % 2]
                total = jnp.sum(total, axis=0, keepdims=True)
                total = jnp.sum(total, axis=1, keepdims=True) / jnp.float32(sites)
                row = row + jnp.where(lanes == k * (nz // 2) + i, total, 0.0)
        return row

    for e in range(1, len(WIDTHS)):
        now, after = buffers[e], (1, 2, None)[e - 1]
        moment = 3 if e == 1 else None
        later = 4 if e == 1 else None
        for k in range(2):
            arrived(e, k, Y_SIDES)
            advance(k, now, 0, 0, x_first + 1, x_end - 1, True, moment)
            sent(e - 1, k)
            advance(k, 0, now, after, x_first + 2, x_end - 2, False, later)
            if e == 3 and k == 0:
                sum_start(2, sum_finish(1))
            arrived(e, k, X_SIDES)
            advance(k, now, 0, 0, x_first - 1, x_first, True)
            advance(k, now, 0, 0, x_first, x_first + 1, True, moment)
            advance(k, 0, now, after, x_first, x_first + 2, False, later)
            advance(k, now, 0, 0, x_end - 1, x_end, True, moment)
            advance(k, now, 0, 0, x_end, x_end + 1, True)
            advance(k, 0, now, after, x_end - 2, x_end, False, later)
            if e + 1 < len(WIDTHS):
                send(e + 1, k)
            if e == 2 and k == 0:
                sum_start(1, sum_finish(0))
        if e == 1:
            sum_start(0, own_moments())

    row = sum_finish(2)
    moments_ref[0:1, :] = row[:, : ITERS + 1]
    moments_ref[1:2, :] = pltpu.roll(row, nz // 2, 1)[:, : ITERS + 1]
    sent(0, 2)
    for k in range(2):
        sent(len(WIDTHS) - 1, k)
    for turn in range(3):
        others = partial.at[turn, pl.ds(0, GROUP - 1)]
        pltpu.make_async_copy(others, others, sum_send.at[turn]).wait()


def local(random_vectors, disorder):
    vectors, nx, ny, nz = random_vectors.shape
    padded = (nx + 2 * HALO, ny + 2 * ROW0, nz)
    return pl.pallas_call(
        body,
        out_shape=(
            pltpu.VMEM((vectors, ITERS + 1), jnp.float32),
            pltpu.VMEM(random_vectors.shape, jnp.float32),
        ),
        in_specs=[pl.BlockSpec(memory_space=pltpu.HBM)] * 2,
        out_specs=(pl.BlockSpec(memory_space=pltpu.VMEM), pl.BlockSpec(memory_space=pltpu.VMEM)),
        scratch_shapes=[
            pltpu.VMEM((vectors, 3, *padded), jnp.float32),
            pltpu.VMEM(padded, jnp.float32),
            pltpu.VMEM((vectors, ITERS + 1, TILE, nz), jnp.float32),
            pltpu.VMEM((3, GROUP, 1, nz), jnp.float32),
            pltpu.SemaphoreType.DMA((3,)),
            pltpu.SemaphoreType.DMA((PARITIES, vectors + 1)),
            pltpu.SemaphoreType.DMA((PARITIES, vectors + 1, 2)),
            pltpu.SemaphoreType.DMA((3,)),
            pltpu.SemaphoreType.DMA((3,)),
        ],
        compiler_params=pltpu.CompilerParams(collective_id=0, has_side_effects=True, vmem_limit_bytes=60 * 2**20),
    )(random_vectors, disorder)


def solution(mesh):
    placed = (P(None, "gx", "gy", None), P("gx", "gy", None))
    return jax.shard_map(
        local,
        mesh=mesh,
        in_specs=placed,
        out_specs=(P(), P(None, "gx", "gy", None)),
        check_vma=False,
    )
```

```python
import functools

import jax
import jax.numpy as jnp
from jax import lax
from jax.experimental import pallas as pl
from jax.experimental.pallas import tpu as pltpu
from jax.sharding import PartitionSpec as P

MESH = pl.DeviceIdType.MESH
ITERS = 9
ENERGY_SCALE = 10.5
TILE = 8
HALO = 2
ROW0 = 2 * TILE
PARITIES = 2
WIDTHS = (1, 2, 2, 2, 2)
SIDES = ((-1, 0), (1, 0), (0, -1), (0, 1), (-1, -1), (-1, 1), (1, -1), (1, 1))
X_SIDES = (0, 1, 4, 5, 6, 7)
Y_SIDES = (2, 3)
GROUP = 8


def body(start_ref, disorder_ref, moments_ref, last_ref, v, energy, sums, partial, local_sem, send_sem, recv_sem, sum_send, sum_recv):
    _, nx, ny, nz = start_ref.shape
    sx, sy = lax.axis_size("gx"), lax.axis_size("gy")
    gx, gy = lax.axis_index("gx"), lax.axis_index("gy")
    x_first, x_end = HALO, HALO + nx
    y_end = ROW0 + ny
    sites = nx * ny * nz * sx * sy

    def beside(dx, dy):
        return (lax.rem(gx + sx + dx, sx), lax.rem(gy + sy + dy, sy))

    z, y_hi = gx // 4, gx % 4
    y_lo, xc = gy // GROUP, gy % GROUP
    y = y_hi * 2 + y_lo
    places = (xc, y, z)

    def partner(turn, d):
        if turn == 0:
            return (gx, y_lo * GROUP + (xc + d) % GROUP)
        if turn == 1:
            to = (y + d) % GROUP
            return (z * 4 + to // 2, (to % 2) * GROUP + xc)
        return (((z + d) % GROUP) * 4 + y_hi, gy)

    barrier = pltpu.get_barrier_semaphore()
    for dx, dy in reversed(SIDES):
        pl.semaphore_signal(barrier, inc=1, device_id=beside(dx, dy), device_id_type=MESH)
    for turn in reversed(range(3)):
        for d in range(1, GROUP):
            pl.semaphore_signal(barrier, inc=1, device_id=partner(turn, d), device_id_type=MESH)

    own = [pltpu.make_async_copy(start_ref.at[k], v.at[k, 0, pl.ds(x_first, nx), pl.ds(ROW0, ny)], local_sem.at[k]) for k in range(2)]
    own.append(pltpu.make_async_copy(disorder_ref, energy.at[pl.ds(x_first, nx), pl.ds(ROW0, ny)], local_sem.at[2]))
    for copy in own:
        copy.start()
    pl.semaphore_wait(barrier, len(SIDES) + 3 * (GROUP - 1))

    buffers = (0, 1, 2, 1, 2)

    def message(e, k, side):
        dx, dy = SIDES[side]
        width = WIDTHS[e] - (dx != 0 and dy != 0)
        x_from, x_size, x_to = {
            -1: (0, width, x_end),
            0: (0, nx, x_first),
            1: (nx - width, width, x_first - width),
        }[dx]
        y_from, y_size, y_to = {
            -1: (0, width, y_end),
            0: (0, ny, ROW0),
            1: (ny - width, width, ROW0 - width),
        }[dy]
        here = (pl.ds(x_from, x_size), pl.ds(y_from, y_size))
        there = (pl.ds(x_to, x_size), pl.ds(y_to, y_size))
        if k == 2:
            src, dst = disorder_ref.at[here], energy.at[there]
        else:
            b = buffers[e]
            if e == 0:
                src = start_ref.at[(k, *here)]
            else:
                src = v.at[k, b, pl.ds(x_first + x_from, x_size), pl.ds(ROW0 + y_from, y_size)]
            dst = v.at[(k, b, *there)]
        return pltpu.make_async_remote_copy(
            src_ref=src,
            dst_ref=dst,
            send_sem=send_sem.at[e % PARITIES, k],
            recv_sem=recv_sem.at[e % PARITIES, k, int(side in X_SIDES)],
            device_id=beside(dx, dy),
            device_id_type=MESH,
        )

    def sides_of(e, within=range(len(SIDES))):
        return [side for side in within if WIDTHS[e] > 1 or 0 in SIDES[side]]

    def send(e, k):
        for side in reversed(sides_of(e)):
            message(e, k, side).start()

    def rows_of(e, sides):
        total = 0
        for side in sides_of(e, sides):
            dx, dy = SIDES[side]
            width = WIDTHS[e] - (dx != 0 and dy != 0)
            total += (width if dx else nx) * (width if dy else ny)
        return total

    def wait_for(rows, semaphore):
        planes = next(n for n in range(1, v.shape[2]) if rows % n == 0 and rows // n <= v.shape[3])
        whole = v.at[0, 0, pl.ds(0, planes), pl.ds(0, rows // planes)]
        pltpu.make_async_copy(whole, whole, semaphore).wait()

    def arrived(e, k, sides):
        wait_for(rows_of(e, sides), recv_sem.at[e % PARITIES, k, int(sides == X_SIDES)])

    def sent(e, k):
        wait_for(rows_of(e, range(len(SIDES))), send_sem.at[e % PARITIES, k])

    def advance(k, now, before, after, x0, x1, wide, moment=None):
        r0, r1 = (ROW0 - TILE, y_end + TILE) if wide else (ROW0, y_end)
        factor = (1.0 if before is None else 2.0) / ENERGY_SCALE
        layers, rows = pl.ds(x0, x1 - x0), pl.ds(r0, r1 - r0)
        center = v[k, now, layers, rows, :]
        total = v[k, now, pl.ds(x0 + 1, x1 - x0), rows, :] + v[k, now, pl.ds(x0 - 1, x1 - x0), rows, :]
        total = total + v[k, now, layers, pl.ds(r0 + 1, r1 - r0), :] + v[k, now, layers, pl.ds(r0 - 1, r1 - r0), :]
        total = total + pltpu.roll(center, nz - 1, 2) + pltpu.roll(center, 1, 2)
        result = (energy[layers, rows, :] * center - total) * factor
        if before is not None:
            result = result - v[k, before, layers, rows, :]
        if after is None:
            last_ref[k, pl.ds(x0 - x_first, x1 - x0)] = result
        else:
            v[k, after, layers, rows, :] = result
        if moment is not None:
            if wide:
                center, result = center[:, TILE:-TILE], result[:, TILE:-TILE]
            of_own = slice(max(x_first - x0, 0), min(x_end, x1) - x0)
            center, result = center[of_own], result[of_own]
            for i, product in enumerate((center * center, center * result)):
                sums[k, 2 * moment + i] += jnp.sum(product.reshape(-1, TILE, nz), axis=0)

    sums[...] = jnp.zeros_like(sums)
    for k in range(3):
        send(0, k)

    for k in range(2):
        own[k].wait()
        if k == 0:
            own[2].wait()
        arrived(0, k, Y_SIDES)
        advance(k, 0, None, 1, x_first + 1, x_end - 1, False, 0)
        arrived(0, k, X_SIDES)
        advance(k, 0, None, 1, x_first, x_first + 1, False, 0)
        advance(k, 0, None, 1, x_end - 1, x_end, False, 0)
        send(1, k)

    def sum_message(turn, d):
        return pltpu.make_async_remote_copy(
            src_ref=partial.at[turn, places[turn]],
            dst_ref=partial.at[turn, places[turn]],
            send_sem=sum_send.at[turn],
            recv_sem=sum_recv.at[turn],
            device_id=partner(turn, d),
            device_id_type=MESH,
        )

    def sum_start(turn, row):
        partial[turn, places[turn]] = row
        for d in range(1, GROUP):
            sum_message(turn, d).start()

    def sum_finish(turn):
        others = partial.at[turn, pl.ds(0, GROUP - 1)]
        pltpu.make_async_copy(others, others, sum_recv.at[turn]).wait()
        row = partial[turn, 0]
        for place in range(1, GROUP):
            row = row + partial[turn, place]
        return row

    def own_moments():
        lanes = lax.broadcasted_iota(jnp.int32, (1, nz), 1)
        row = jnp.zeros((1, nz), jnp.float32)
        for k in range(2):
            for i in range(ITERS + 1):
                total = sums[k, i]
                if i >= 2:
                    total = 2.0 * total - sums[k, i % 2]
                total = jnp.sum(total, axis=0, keepdims=True)
                total = jnp.sum(total, axis=1, keepdims=True) / jnp.float32(sites)
                row = row + jnp.where(lanes == k * (nz // 2) + i, total, 0.0)
        return row

    for e in range(1, len(WIDTHS)):
        now, after = buffers[e], (2, 1, 2, None)[e - 1]
        moment, later = ((1, 2), (3, 4), (None, None), (None, None))[e - 1]
        for k in range(2):
            if e == 1 and k == 0:
                arrived(0, 2, Y_SIDES)
            arrived(e, k, Y_SIDES)
            advance(k, now, 0, 0, x_first + 1, x_end - 1, True, moment)
            sent(e - 1, k)
            advance(k, 0, now, after, x_first + 2, x_end - 2, False, later)
            if e == 4 and k == 0:
                sum_start(2, sum_finish(1))
            if e == 1 and k == 0:
                arrived(0, 2, X_SIDES)
            arrived(e, k, X_SIDES)
            advance(k, now, 0, 0, x_first - 1, x_first + 1, True, moment)
            advance(k, now, 0, 0, x_end - 1, x_end + 1, True, moment)
            advance(k, 0, now, after, x_first, x_first + 2, False, later)
            advance(k, 0, now, after, x_end - 2, x_end, False, later)
            if e + 1 < len(WIDTHS):
                send(e + 1, k)
            if e == 3 and k == 0:
                sum_start(1, sum_finish(0))
        if e == 2:
            sum_start(0, own_moments())

    row = sum_finish(2)
    moments_ref[0:1, :] = row[:, : ITERS + 1]
    moments_ref[1:2, :] = pltpu.roll(row, nz // 2, 1)[:, : ITERS + 1]
    sent(0, 2)
    for k in range(2):
        sent(len(WIDTHS) - 1, k)
    for turn in range(3):
        others = partial.at[turn, pl.ds(0, GROUP - 1)]
        pltpu.make_async_copy(others, others, sum_send.at[turn]).wait()


def to_hbm(moments_ref, last_ref, moments_out, last_out, sems):
    copies = [pltpu.make_async_copy(moments_ref, moments_out, sems.at[0])]
    copies += [pltpu.make_async_copy(last_ref.at[k], last_out.at[k], sems.at[k + 1]) for k in range(2)]
    for copy in copies:
        copy.start()
    for copy in copies:
        copy.wait()


def local(random_vectors, disorder):
    vectors, nx, ny, nz = random_vectors.shape
    padded = (nx + 2 * HALO, ny + 2 * ROW0, nz)
    outputs = pl.pallas_call(
        body,
        out_shape=(
            pltpu.VMEM((vectors, ITERS + 1), jnp.float32),
            pltpu.VMEM(random_vectors.shape, jnp.float32),
        ),
        in_specs=[pl.BlockSpec(memory_space=pltpu.HBM)] * 2,
        out_specs=(pl.BlockSpec(memory_space=pltpu.VMEM), pl.BlockSpec(memory_space=pltpu.VMEM)),
        scratch_shapes=[
            pltpu.VMEM((vectors, 3, *padded), jnp.float32),
            pltpu.VMEM(padded, jnp.float32),
            pltpu.VMEM((vectors, ITERS + 1, TILE, nz), jnp.float32),
            pltpu.VMEM((3, GROUP, 1, nz), jnp.float32),
            pltpu.SemaphoreType.DMA((3,)),
            pltpu.SemaphoreType.DMA((PARITIES, vectors + 1)),
            pltpu.SemaphoreType.DMA((PARITIES, vectors + 1, 2)),
            pltpu.SemaphoreType.DMA((3,)),
            pltpu.SemaphoreType.DMA((3,)),
        ],
        compiler_params=pltpu.CompilerParams(collective_id=0, has_side_effects=True, vmem_limit_bytes=60 * 2**20),
    )(random_vectors, disorder)
    return pl.pallas_call(
        to_hbm,
        out_shape=(
            jax.ShapeDtypeStruct((vectors, ITERS + 1), jnp.float32),
            jax.ShapeDtypeStruct(random_vectors.shape, jnp.float32),
        ),
        in_specs=[pl.BlockSpec(memory_space=pltpu.VMEM)] * 2,
        out_specs=(pl.BlockSpec(memory_space=pltpu.HBM), pl.BlockSpec(memory_space=pltpu.HBM)),
        scratch_shapes=[pltpu.SemaphoreType.DMA((vectors + 1,))],
        compiler_params=pltpu.CompilerParams(vmem_limit_bytes=2**20),
    )(*outputs)


def solution(mesh):
    placed = (P(None, "gx", "gy", None), P("gx", "gy", None))
    return jax.shard_map(
        local,
        mesh=mesh,
        in_specs=placed,
        out_specs=(P(), P(None, "gx", "gy", None)),
        check_vma=False,
    )
```

```python
import functools

import jax
import jax.numpy as jnp
from jax import lax
from jax.experimental import pallas as pl
from jax.experimental.pallas import tpu as pltpu
from jax.sharding import PartitionSpec as P

MESH = pl.DeviceIdType.MESH
ITERS = 9
ENERGY_SCALE = 10.5
TILE = 8
HALO = 2
ROW0 = 2 * TILE
PARITIES = 2
WIDTHS = (1, 2, 2, 2, 2)
ENDS = (0, 18, 17, 16, 15)
SIDES = ((-1, 0), (1, 0), (0, -1), (0, 1), (-1, -1), (-1, 1), (1, -1), (1, 1))
X_SIDES = (0, 1, 4, 5, 6, 7)
Y_SIDES = (2, 3)
X_FACES = (0, 1)
GROUP = 8


def body(start_ref, disorder_ref, moments_ref, last_ref, v, energy, sums, partial, local_sem, send_sem, recv_sem, sum_send, sum_recv):
    _, nx, ny, nz = start_ref.shape
    sx, sy = lax.axis_size("gx"), lax.axis_size("gy")
    gx, gy = lax.axis_index("gx"), lax.axis_index("gy")
    x_first, x_end = HALO, HALO + nx
    y_end = ROW0 + ny
    sites = nx * ny * nz * sx * sy

    def beside(dx, dy):
        return (lax.rem(gx + sx + dx, sx), lax.rem(gy + sy + dy, sy))

    z, y_hi = gx // 4, gx % 4
    y_lo, xc = gy // GROUP, gy % GROUP
    y = y_hi * 2 + y_lo
    places = (xc, y, z)

    def partner(turn, d):
        if turn == 0:
            return (gx, y_lo * GROUP + (xc + d) % GROUP)
        if turn == 1:
            to = (y + d) % GROUP
            return (z * 4 + to // 2, (to % 2) * GROUP + xc)
        return (((z + d) % GROUP) * 4 + y_hi, gy)

    barrier = pltpu.get_barrier_semaphore()
    for dx, dy in reversed(SIDES):
        pl.semaphore_signal(barrier, inc=1, device_id=beside(dx, dy), device_id_type=MESH)
    for turn in reversed(range(3)):
        for d in range(1, GROUP):
            pl.semaphore_signal(barrier, inc=1, device_id=partner(turn, d), device_id_type=MESH)

    own = [pltpu.make_async_copy(start_ref.at[k], v.at[k, 0, pl.ds(x_first, nx), pl.ds(ROW0, ny)], local_sem.at[k]) for k in range(2)]
    own.append(pltpu.make_async_copy(disorder_ref, energy.at[pl.ds(x_first, nx), pl.ds(ROW0, ny)], local_sem.at[2]))
    for copy in own:
        copy.start()
    pl.semaphore_wait(barrier, len(SIDES) + 3 * (GROUP - 1))

    buffers = (0, 1, 2, 1, 2)

    def message(e, k, side, part=None):
        dx, dy = SIDES[side]
        width = WIDTHS[e] - (dx != 0 and dy != 0)
        x_from, x_size, x_to = {
            -1: (0, width, x_end),
            0: (0, nx, x_first),
            1: (nx - width, width, x_first - width),
        }[dx]
        y_from, y_size, y_to = {
            -1: (0, width, y_end),
            0: (0, ny, ROW0),
            1: (ny - width, width, ROW0 - width),
        }[dy]
        if part is not None:
            y_from, y_size = ((0, ENDS[e]), (ny - ENDS[e], ENDS[e]), (ENDS[e], ny - 2 * ENDS[e]))[part]
            y_to = ROW0 + y_from
        here = (pl.ds(x_from, x_size), pl.ds(y_from, y_size))
        there = (pl.ds(x_to, x_size), pl.ds(y_to, y_size))
        if k == 2:
            src, dst = disorder_ref.at[here], energy.at[there]
        else:
            b = buffers[e]
            if e == 0:
                src = start_ref.at[(k, *here)]
            else:
                src = v.at[k, b, pl.ds(x_first + x_from, x_size), pl.ds(ROW0 + y_from, y_size)]
            dst = v.at[(k, b, *there)]
        return pltpu.make_async_remote_copy(
            src_ref=src,
            dst_ref=dst,
            send_sem=send_sem.at[e % PARITIES, k],
            recv_sem=recv_sem.at[e % PARITIES, k, 2 if part == 2 else int(side in X_SIDES)],
            device_id=beside(dx, dy),
            device_id_type=MESH,
        )

    def sides_of(e, within=range(len(SIDES))):
        return [side for side in within if WIDTHS[e] > 1 or 0 in SIDES[side]]

    def send(e, k):
        for side in reversed(sides_of(e)):
            if e > 0 and side in X_FACES:
                for part in range(2):
                    message(e, k, side, part).start()
            else:
                message(e, k, side).start()

    def send_middle(e, k):
        for side in X_FACES:
            message(e, k, side, 2).start()

    def rows_of(e, sides):
        total = 0
        for side in sides_of(e, sides):
            dx, dy = SIDES[side]
            width = WIDTHS[e] - (dx != 0 and dy != 0)
            total += (width if dx else nx) * (width if dy else ny)
        return total

    def wait_for(rows, semaphore):
        planes = next(n for n in range(1, v.shape[2]) if rows % n == 0 and rows // n <= v.shape[3])
        whole = v.at[0, 0, pl.ds(0, planes), pl.ds(0, rows // planes)]
        pltpu.make_async_copy(whole, whole, semaphore).wait()

    def middle_rows(e):
        return 2 * WIDTHS[e] * (ny - 2 * ENDS[e]) if e > 0 else 0

    def arrived(e, k, sides):
        rows = rows_of(e, sides) - (middle_rows(e) if sides == X_SIDES else 0)
        wait_for(rows, recv_sem.at[e % PARITIES, k, int(sides == X_SIDES)])

    def middle_arrived(e, k):
        wait_for(middle_rows(e), recv_sem.at[e % PARITIES, k, 2])

    def sent(e, k):
        wait_for(rows_of(e, range(len(SIDES))), send_sem.at[e % PARITIES, k])

    def advance(k, now, before, after, x0, x1, wide, moment=None, between=None):
        r0, r1 = between or ((ROW0 - TILE, y_end + TILE) if wide else (ROW0, y_end))
        factor = (1.0 if before is None else 2.0) / ENERGY_SCALE
        layers, rows = pl.ds(x0, x1 - x0), pl.ds(r0, r1 - r0)
        center = v[k, now, layers, rows, :]
        total = v[k, now, pl.ds(x0 + 1, x1 - x0), rows, :] + v[k, now, pl.ds(x0 - 1, x1 - x0), rows, :]
        total = total + v[k, now, layers, pl.ds(r0 + 1, r1 - r0), :] + v[k, now, layers, pl.ds(r0 - 1, r1 - r0), :]
        total = total + pltpu.roll(center, nz - 1, 2) + pltpu.roll(center, 1, 2)
        result = (energy[layers, rows, :] * center - total) * factor
        if before is not None:
            result = result - v[k, before, layers, rows, :]
        if after is None:
            last_ref[k, pl.ds(x0 - x_first, x1 - x0)] = result
        else:
            v[k, after, layers, rows, :] = result
        if moment is not None:
            if wide:
                center, result = center[:, TILE:-TILE], result[:, TILE:-TILE]
            of_own = slice(max(x_first - x0, 0), min(x_end, x1) - x0)
            center, result = center[of_own], result[of_own]
            add_moments(k, moment, center, result)

    def add_moments(k, moment, center, result):
        for i, product in enumerate((center * center, center * result)):
            sums[k, 2 * moment + i] += jnp.sum(product.reshape(-1, TILE, nz), axis=0)

    def record(k, now, after, x0, x1, moment):
        at = (pl.ds(x0, x1 - x0), pl.ds(ROW0, ny))
        add_moments(k, moment, v[(k, now, *at)], v[(k, after, *at)])

    def edges(k, now, after, spans_outer, spans_first, spans_next):
        for spans, layers in ((spans_outer, (x_first - 1, x_end)), (spans_first, (x_first, x_end - 1))):
            for x in layers:
                for span in spans:
                    advance(k, now, 0, 0, x, x + 1, False, between=span)
        for x in (x_first, x_end - 2):
            for span in spans_next:
                advance(k, 0, now, after, x, x + 2, False, between=span)

    sums[...] = jnp.zeros_like(sums)
    for k in (0, 2, 1):
        send(0, k)

    for k in range(2):
        own[k].wait()
        if k == 0:
            own[2].wait()
        arrived(0, k, Y_SIDES)
        advance(k, 0, None, 1, x_first + 1, x_end - 1, False, 0)
        arrived(0, k, X_SIDES)
        advance(k, 0, None, 1, x_first, x_first + 1, False, 0)
        advance(k, 0, None, 1, x_end - 1, x_end, False, 0)
        send(1, k)
        send_middle(1, k)

    def sum_message(turn, d):
        return pltpu.make_async_remote_copy(
            src_ref=partial.at[turn, places[turn]],
            dst_ref=partial.at[turn, places[turn]],
            send_sem=sum_send.at[turn],
            recv_sem=sum_recv.at[turn],
            device_id=partner(turn, d),
            device_id_type=MESH,
        )

    def sum_start(turn, row):
        partial[turn, places[turn]] = row
        for d in range(1, GROUP):
            sum_message(turn, d).start()

    def sum_finish(turn):
        others = partial.at[turn, pl.ds(0, GROUP - 1)]
        pltpu.make_async_copy(others, others, sum_recv.at[turn]).wait()
        row = partial[turn, 0]
        for place in range(1, GROUP):
            row = row + partial[turn, place]
        return row

    def own_moments():
        lanes = lax.broadcasted_iota(jnp.int32, (1, nz), 1)
        row = jnp.zeros((1, nz), jnp.float32)
        for k in range(2):
            for i in range(ITERS + 1):
                total = sums[k, i]
                if i >= 2:
                    total = 2.0 * total - sums[k, i % 2]
                total = jnp.sum(total, axis=0, keepdims=True)
                total = jnp.sum(total, axis=1, keepdims=True) / jnp.float32(sites)
                row = row + jnp.where(lanes == k * (nz // 2) + i, total, 0.0)
        return row

    for e in range(1, len(WIDTHS)):
        now, after = buffers[e], (2, 1, 2, None)[e - 1]
        moment, later = ((1, 2), (3, 4), (None, None), (None, None))[e - 1]
        for k in range(2):
            if e == 1 and k == 0:
                arrived(0, 2, Y_SIDES)
            arrived(e, k, Y_SIDES)
            advance(k, now, 0, 0, x_first + 1, x_end - 1, True, moment)
            sent(e - 1, k)
            advance(k, 0, now, after, x_first + 2, x_end - 2, False, later)
            if e == 4 and k == 0:
                sum_start(2, sum_finish(1))
            if e == 1 and k == 0:
                arrived(0, 2, X_SIDES)
            arrived(e, k, X_SIDES)
            if e + 1 < len(WIDTHS):
                low, high = ROW0 + ENDS[e + 1], y_end - ENDS[e + 1]
                ends = ((ROW0, low), (high, y_end))
                edges(k, now, after, ends, ((ROW0 - TILE, low + 1), (high - 1, y_end + TILE)), ends)
                send(e + 1, k)
                middle_arrived(e, k)
                edges(k, now, after, ((low, high),), ((low + 1, high - 1),), ((low, high),))
                send_middle(e + 1, k)
                if moment is not None:
                    for x in (x_first, x_end - 1):
                        record(k, now, 0, x, x + 1, moment)
                    for x in (x_first, x_end - 2):
                        record(k, 0, after, x, x + 2, later)
            else:
                middle_arrived(e, k)
                advance(k, now, 0, 0, x_first - 1, x_first + 1, True)
                advance(k, now, 0, 0, x_end - 1, x_end + 1, True)
                advance(k, 0, now, after, x_first, x_first + 2, False)
                advance(k, 0, now, after, x_end - 2, x_end, False)
            if e == 3 and k == 0:
                sum_start(1, sum_finish(0))
        if e == 2:
            sum_start(0, own_moments())

    row = sum_finish(2)
    moments_ref[0:1, :] = row[:, : ITERS + 1]
    moments_ref[1:2, :] = pltpu.roll(row, nz // 2, 1)[:, : ITERS + 1]
    sent(0, 2)
    for k in range(2):
        sent(len(WIDTHS) - 1, k)
    for turn in range(3):
        others = partial.at[turn, pl.ds(0, GROUP - 1)]
        pltpu.make_async_copy(others, others, sum_send.at[turn]).wait()


def to_hbm(moments_ref, last_ref, moments_out, last_out, sems):
    copies = [pltpu.make_async_copy(moments_ref, moments_out, sems.at[0])]
    copies += [pltpu.make_async_copy(last_ref.at[k], last_out.at[k], sems.at[k + 1]) for k in range(2)]
    for copy in copies:
        copy.start()
    for copy in copies:
        copy.wait()


def local(random_vectors, disorder):
    vectors, nx, ny, nz = random_vectors.shape
    padded = (nx + 2 * HALO, ny + 2 * ROW0, nz)
    outputs = pl.pallas_call(
        body,
        out_shape=(
            pltpu.VMEM((vectors, ITERS + 1), jnp.float32),
            pltpu.VMEM(random_vectors.shape, jnp.float32),
        ),
        in_specs=[pl.BlockSpec(memory_space=pltpu.HBM)] * 2,
        out_specs=(pl.BlockSpec(memory_space=pltpu.VMEM), pl.BlockSpec(memory_space=pltpu.VMEM)),
        scratch_shapes=[
            pltpu.VMEM((vectors, 3, *padded), jnp.float32),
            pltpu.VMEM(padded, jnp.float32),
            pltpu.VMEM((vectors, ITERS + 1, TILE, nz), jnp.float32),
            pltpu.VMEM((3, GROUP, 1, nz), jnp.float32),
            pltpu.SemaphoreType.DMA((3,)),
            pltpu.SemaphoreType.DMA((PARITIES, vectors + 1)),
            pltpu.SemaphoreType.DMA((PARITIES, vectors + 1, 3)),
            pltpu.SemaphoreType.DMA((3,)),
            pltpu.SemaphoreType.DMA((3,)),
        ],
        compiler_params=pltpu.CompilerParams(collective_id=0, has_side_effects=True, vmem_limit_bytes=60 * 2**20),
    )(random_vectors, disorder)
    return pl.pallas_call(
        to_hbm,
        out_shape=(
            jax.ShapeDtypeStruct((vectors, ITERS + 1), jnp.float32),
            jax.ShapeDtypeStruct(random_vectors.shape, jnp.float32),
        ),
        in_specs=[pl.BlockSpec(memory_space=pltpu.VMEM)] * 2,
        out_specs=(pl.BlockSpec(memory_space=pltpu.HBM), pl.BlockSpec(memory_space=pltpu.HBM)),
        scratch_shapes=[pltpu.SemaphoreType.DMA((vectors + 1,))],
        compiler_params=pltpu.CompilerParams(vmem_limit_bytes=2**20),
    )(*outputs)


def solution(mesh):
    placed = (P(None, "gx", "gy", None), P("gx", "gy", None))
    return jax.shard_map(
        local,
        mesh=mesh,
        in_specs=placed,
        out_specs=(P(), P(None, "gx", "gy", None)),
        check_vma=False,
    )
```

```python
import functools

import jax
import jax.numpy as jnp
from jax import lax
from jax.experimental import pallas as pl
from jax.experimental.pallas import tpu as pltpu
from jax.sharding import PartitionSpec as P

MESH = pl.DeviceIdType.MESH
ITERS = 9
ENERGY_SCALE = 10.5
TILE = 8
HALO = 2
ROW0 = 2 * TILE
PARITIES = 2
WIDTHS = (1, 2, 2, 2, 2)
ENDS = (0, 18, 17, 16, 15)
SIDES = ((-1, 0), (1, 0), (0, -1), (0, 1), (-1, -1), (-1, 1), (1, -1), (1, 1))
X_SIDES = (0, 1, 4, 5, 6, 7)
Y_SIDES = (2, 3)
X_FACES = (0, 1)
GROUP = 8


def body(start_ref, disorder_ref, moments_ref, last_ref, v, energy, sums, partial, local_sem, send_sem, recv_sem, sum_send, sum_recv):
    _, nx, ny, nz = start_ref.shape
    sx, sy = lax.axis_size("gx"), lax.axis_size("gy")
    gx, gy = lax.axis_index("gx"), lax.axis_index("gy")
    x_first, x_end = HALO, HALO + nx
    y_end = ROW0 + ny
    sites = nx * ny * nz * sx * sy

    def beside(dx, dy):
        return (lax.rem(gx + sx + dx, sx), lax.rem(gy + sy + dy, sy))

    z, y_hi = gx // 4, gx % 4
    y_lo, xc = gy // GROUP, gy % GROUP
    y = y_hi * 2 + y_lo
    places = (xc, y, z)

    def partner(turn, d):
        if turn == 0:
            return (gx, y_lo * GROUP + (xc + d) % GROUP)
        if turn == 1:
            to = (y + d) % GROUP
            return (z * 4 + to // 2, (to % 2) * GROUP + xc)
        return (((z + d) % GROUP) * 4 + y_hi, gy)

    barrier = pltpu.get_barrier_semaphore()
    for dx, dy in reversed(SIDES):
        pl.semaphore_signal(barrier, inc=1, device_id=beside(dx, dy), device_id_type=MESH)
    for turn in reversed(range(3)):
        for d in range(1, GROUP):
            pl.semaphore_signal(barrier, inc=1, device_id=partner(turn, d), device_id_type=MESH)

    own = [pltpu.make_async_copy(start_ref.at[k], v.at[k, 0, pl.ds(x_first, nx), pl.ds(ROW0, ny)], local_sem.at[k]) for k in range(2)]
    own.append(pltpu.make_async_copy(disorder_ref, energy.at[pl.ds(x_first, nx), pl.ds(ROW0, ny)], local_sem.at[2]))
    for copy in own:
        copy.start()
    pl.semaphore_wait(barrier, len(SIDES) + 3 * (GROUP - 1))

    buffers = (0, 1, 2, 1, 2)

    def message(e, k, side, part=None):
        dx, dy = SIDES[side]
        width = WIDTHS[e] - (dx != 0 and dy != 0)
        x_from, x_size, x_to = {
            -1: (0, width, x_end),
            0: (0, nx, x_first),
            1: (nx - width, width, x_first - width),
        }[dx]
        y_from, y_size, y_to = {
            -1: (0, width, y_end),
            0: (0, ny, ROW0),
            1: (ny - width, width, ROW0 - width),
        }[dy]
        if part is not None:
            y_from, y_size = ((0, ENDS[e]), (ny - ENDS[e], ENDS[e]), (ENDS[e], ny - 2 * ENDS[e]))[part]
            y_to = ROW0 + y_from
        here = (pl.ds(x_from, x_size), pl.ds(y_from, y_size))
        there = (pl.ds(x_to, x_size), pl.ds(y_to, y_size))
        if k == 2:
            src, dst = disorder_ref.at[here], energy.at[there]
        else:
            b = buffers[e]
            if e == 0:
                src = start_ref.at[(k, *here)]
            else:
                src = v.at[k, b, pl.ds(x_first + x_from, x_size), pl.ds(ROW0 + y_from, y_size)]
            dst = v.at[(k, b, *there)]
        return pltpu.make_async_remote_copy(
            src_ref=src,
            dst_ref=dst,
            send_sem=send_sem.at[e % PARITIES, k],
            recv_sem=recv_sem.at[e % PARITIES, k, 2 if part == 2 else int(side in X_SIDES)],
            device_id=beside(dx, dy),
            device_id_type=MESH,
        )

    def sides_of(e, within=range(len(SIDES))):
        return [side for side in within if WIDTHS[e] > 1 or 0 in SIDES[side]]

    def send(e, k):
        for side in reversed(sides_of(e)):
            if e > 0 and side in X_FACES:
                for part in range(2):
                    message(e, k, side, part).start()
            else:
                message(e, k, side).start()

    def send_middle(e, k):
        for side in X_FACES:
            message(e, k, side, 2).start()

    def rows_of(e, sides):
        total = 0
        for side in sides_of(e, sides):
            dx, dy = SIDES[side]
            width = WIDTHS[e] - (dx != 0 and dy != 0)
            total += (width if dx else nx) * (width if dy else ny)
        return total

    def wait_for(rows, semaphore):
        planes = next(n for n in range(1, v.shape[2]) if rows % n == 0 and rows // n <= v.shape[3])
        whole = v.at[0, 0, pl.ds(0, planes), pl.ds(0, rows // planes)]
        pltpu.make_async_copy(whole, whole, semaphore).wait()

    def middle_rows(e):
        return 2 * WIDTHS[e] * (ny - 2 * ENDS[e]) if e > 0 else 0

    def arrived(e, k, sides):
        rows = rows_of(e, sides) - (middle_rows(e) if sides == X_SIDES else 0)
        wait_for(rows, recv_sem.at[e % PARITIES, k, int(sides == X_SIDES)])

    def middle_arrived(e, k):
        wait_for(middle_rows(e), recv_sem.at[e % PARITIES, k, 2])

    def sent(e, k):
        wait_for(rows_of(e, range(len(SIDES))), send_sem.at[e % PARITIES, k])

    def advance(k, now, before, after, x0, x1, wide, moment=None, between=None):
        r0, r1 = between or ((ROW0 - TILE, y_end + TILE) if wide else (ROW0, y_end))
        factor = (1.0 if before is None else 2.0) / ENERGY_SCALE
        layers, rows = pl.ds(x0, x1 - x0), pl.ds(r0, r1 - r0)
        center = v[k, now, layers, rows, :]
        total = v[k, now, pl.ds(x0 + 1, x1 - x0), rows, :] + v[k, now, pl.ds(x0 - 1, x1 - x0), rows, :]
        total = total + v[k, now, layers, pl.ds(r0 + 1, r1 - r0), :] + v[k, now, layers, pl.ds(r0 - 1, r1 - r0), :]
        total = total + pltpu.roll(center, nz - 1, 2) + pltpu.roll(center, 1, 2)
        result = (energy[layers, rows, :] * center - total) * factor
        if before is not None:
            result = result - v[k, before, layers, rows, :]
        if after is None:
            last_ref[k, pl.ds(x0 - x_first, x1 - x0)] = result
        else:
            v[k, after, layers, rows, :] = result
        if moment is not None:
            if wide:
                center, result = center[:, TILE:-TILE], result[:, TILE:-TILE]
            of_own = slice(max(x_first - x0, 0), min(x_end, x1) - x0)
            center, result = center[of_own], result[of_own]
            add_moments(k, moment, center, result)

    def add_moments(k, moment, center, result):
        for i, product in enumerate((center * center, center * result)):
            sums[k, 2 * moment + i] += jnp.sum(product.reshape(-1, TILE, nz), axis=0)

    def record(k, now, after, x0, x1, moment):
        at = (pl.ds(x0, x1 - x0), pl.ds(ROW0, ny))
        add_moments(k, moment, v[(k, now, *at)], v[(k, after, *at)])

    def edges(k, now, after, spans_outer, spans_first, spans_next):
        for spans, layers in ((spans_outer, (x_first - 1, x_end)), (spans_first, (x_first, x_end - 1))):
            for x in layers:
                for span in spans:
                    advance(k, now, 0, 0, x, x + 1, False, between=span)
        for x in (x_first, x_end - 2):
            for span in spans_next:
                advance(k, 0, now, after, x, x + 2, False, between=span)

    sums[...] = jnp.zeros_like(sums)
    for k in (0, 2, 1):
        send(0, k)

    for k in range(2):
        own[k].wait()
        if k == 0:
            own[2].wait()
        arrived(0, k, Y_SIDES)
        advance(k, 0, None, 1, x_first + 1, x_end - 1, False, 0)
        arrived(0, k, X_SIDES)
        advance(k, 0, None, 1, x_first, x_first + 1, False, 0)
        advance(k, 0, None, 1, x_end - 1, x_end, False, 0)
        send(1, k)
        send_middle(1, k)

    def sum_message(turn, d):
        return pltpu.make_async_remote_copy(
            src_ref=partial.at[turn, places[turn]],
            dst_ref=partial.at[turn, places[turn]],
            send_sem=sum_send.at[turn],
            recv_sem=sum_recv.at[turn],
            device_id=partner(turn, d),
            device_id_type=MESH,
        )

    def sum_start(turn, row):
        partial[turn, places[turn]] = row
        for d in range(1, GROUP):
            sum_message(turn, d).start()

    def sum_finish(turn):
        others = partial.at[turn, pl.ds(0, GROUP - 1)]
        pltpu.make_async_copy(others, others, sum_recv.at[turn]).wait()
        row = partial[turn, 0]
        for place in range(1, GROUP):
            row = row + partial[turn, place]
        return row

    def own_moments():
        lanes = lax.broadcasted_iota(jnp.int32, (1, nz), 1)
        row = jnp.zeros((1, nz), jnp.float32)
        for k in range(2):
            for i in range(ITERS + 1):
                total = sums[k, i]
                if i >= 2:
                    total = 2.0 * total - sums[k, i % 2]
                total = jnp.sum(total, axis=0, keepdims=True)
                total = jnp.sum(total, axis=1, keepdims=True) / jnp.float32(sites)
                row = row + jnp.where(lanes == k * (nz // 2) + i, total, 0.0)
        return row

    for e in range(1, len(WIDTHS)):
        now, after = buffers[e], (2, 1, 2, None)[e - 1]
        moment, later = ((1, 2), (3, 4), (None, None), (None, None))[e - 1]
        for k in range(2):
            if e == 1 and k == 0:
                arrived(0, 2, Y_SIDES)
            arrived(e, k, Y_SIDES)
            advance(k, now, 0, 0, x_first + 1, x_end - 1, True, moment)
            sent(e - 1, k)
            advance(k, 0, now, after, x_first + 2, x_end - 2, False, later)
            if e == 4 and k == 0:
                sum_start(2, sum_finish(1))
            if e == 1 and k == 0:
                arrived(0, 2, X_SIDES)
            arrived(e, k, X_SIDES)
            if e + 1 < len(WIDTHS):
                low, high = ROW0 + ENDS[e + 1], y_end - ENDS[e + 1]
                ends = ((ROW0, low), (high, y_end))
                edges(k, now, after, ends, ((ROW0 - TILE, low + 1), (high - 1, y_end + TILE)), ends)
                send(e + 1, k)
                if e == 3 and k == 0:
                    sum_start(1, sum_finish(0))
                middle_arrived(e, k)
                edges(k, now, after, ((low, high),), ((low + 1, high - 1),), ((low, high),))
                send_middle(e + 1, k)
                if moment is not None:
                    for x in (x_first, x_end - 1):
                        record(k, now, 0, x, x + 1, moment)
                    for x in (x_first, x_end - 2):
                        record(k, 0, after, x, x + 2, later)
            else:
                middle_arrived(e, k)
                advance(k, now, 0, 0, x_first - 1, x_first + 1, True)
                advance(k, now, 0, 0, x_end - 1, x_end + 1, True)
                advance(k, 0, now, after, x_first, x_first + 2, False)
                advance(k, 0, now, after, x_end - 2, x_end, False)
        if e == 2:
            sum_start(0, own_moments())

    row = sum_finish(2)
    moments_ref[0:1, :] = row[:, : ITERS + 1]
    moments_ref[1:2, :] = pltpu.roll(row, nz // 2, 1)[:, : ITERS + 1]
    sent(0, 2)
    for k in range(2):
        sent(len(WIDTHS) - 1, k)
    for turn in range(3):
        others = partial.at[turn, pl.ds(0, GROUP - 1)]
        pltpu.make_async_copy(others, others, sum_send.at[turn]).wait()


def to_hbm(moments_ref, last_ref, moments_out, last_out, sems):
    copies = [pltpu.make_async_copy(moments_ref, moments_out, sems.at[0])]
    copies += [pltpu.make_async_copy(last_ref.at[k], last_out.at[k], sems.at[k + 1]) for k in range(2)]
    for copy in copies:
        copy.start()
    for copy in copies:
        copy.wait()


def local(random_vectors, disorder):
    vectors, nx, ny, nz = random_vectors.shape
    padded = (nx + 2 * HALO, ny + 2 * ROW0, nz)
    outputs = pl.pallas_call(
        body,
        out_shape=(
            pltpu.VMEM((vectors, ITERS + 1), jnp.float32),
            pltpu.VMEM(random_vectors.shape, jnp.float32),
        ),
        in_specs=[pl.BlockSpec(memory_space=pltpu.HBM)] * 2,
        out_specs=(pl.BlockSpec(memory_space=pltpu.VMEM), pl.BlockSpec(memory_space=pltpu.VMEM)),
        scratch_shapes=[
            pltpu.VMEM((vectors, 3, *padded), jnp.float32),
            pltpu.VMEM(padded, jnp.float32),
            pltpu.VMEM((vectors, ITERS + 1, TILE, nz), jnp.float32),
            pltpu.VMEM((3, GROUP, 1, nz), jnp.float32),
            pltpu.SemaphoreType.DMA((3,)),
            pltpu.SemaphoreType.DMA((PARITIES, vectors + 1)),
            pltpu.SemaphoreType.DMA((PARITIES, vectors + 1, 3)),
            pltpu.SemaphoreType.DMA((3,)),
            pltpu.SemaphoreType.DMA((3,)),
        ],
        compiler_params=pltpu.CompilerParams(collective_id=0, has_side_effects=True, vmem_limit_bytes=60 * 2**20),
    )(random_vectors, disorder)
    return pl.pallas_call(
        to_hbm,
        out_shape=(
            jax.ShapeDtypeStruct((vectors, ITERS + 1), jnp.float32),
            jax.ShapeDtypeStruct(random_vectors.shape, jnp.float32),
        ),
        in_specs=[pl.BlockSpec(memory_space=pltpu.VMEM)] * 2,
        out_specs=(pl.BlockSpec(memory_space=pltpu.HBM), pl.BlockSpec(memory_space=pltpu.HBM)),
        scratch_shapes=[pltpu.SemaphoreType.DMA((vectors + 1,))],
        compiler_params=pltpu.CompilerParams(vmem_limit_bytes=2**20),
    )(*outputs)


def solution(mesh):
    placed = (P(None, "gx", "gy", None), P("gx", "gy", None))
    return jax.shard_map(
        local,
        mesh=mesh,
        in_specs=placed,
        out_specs=(P(), P(None, "gx", "gy", None)),
        check_vma=False,
    )
```

```python
import functools

import jax
import jax.numpy as jnp
from jax import lax
from jax.experimental import pallas as pl
from jax.experimental.pallas import tpu as pltpu
from jax.sharding import PartitionSpec as P

MESH = pl.DeviceIdType.MESH
ITERS = 9
ENERGY_SCALE = 10.5
TILE = 8
HALO = 2
ROW0 = 2 * TILE
PARITIES = 2
WIDTHS = (1, 2, 2, 2, 2)
ENDS = (0, 18, 17, 16, 15, 14)
SIDES = ((-1, 0), (1, 0), (0, -1), (0, 1), (-1, -1), (-1, 1), (1, -1), (1, 1))
X_SIDES = (0, 1, 4, 5, 6, 7)
Y_SIDES = (2, 3)
X_FACES = (0, 1)
GROUP = 8


def body(start_ref, disorder_ref, moments_ref, last_ref, v, energy, sums, partial, local_sem, send_sem, recv_sem, sum_send, sum_recv):
    _, nx, ny, nz = start_ref.shape
    sx, sy = lax.axis_size("gx"), lax.axis_size("gy")
    gx, gy = lax.axis_index("gx"), lax.axis_index("gy")
    x_first, x_end = HALO, HALO + nx
    y_end = ROW0 + ny
    sites = nx * ny * nz * sx * sy

    def beside(dx, dy):
        return (lax.rem(gx + sx + dx, sx), lax.rem(gy + sy + dy, sy))

    z, y_hi = gx // 4, gx % 4
    y_lo, xc = gy // GROUP, gy % GROUP
    y = y_hi * 2 + y_lo
    places = (xc, y, z)

    def partner(turn, d):
        if turn == 0:
            return (gx, y_lo * GROUP + (xc + d) % GROUP)
        if turn == 1:
            to = (y + d) % GROUP
            return (z * 4 + to // 2, (to % 2) * GROUP + xc)
        return (((z + d) % GROUP) * 4 + y_hi, gy)

    barrier = pltpu.get_barrier_semaphore()
    for dx, dy in reversed(SIDES):
        pl.semaphore_signal(barrier, inc=1, device_id=beside(dx, dy), device_id_type=MESH)
    for turn in reversed(range(3)):
        for d in range(1, GROUP):
            pl.semaphore_signal(barrier, inc=1, device_id=partner(turn, d), device_id_type=MESH)

    own = [pltpu.make_async_copy(start_ref.at[k], v.at[k, 0, pl.ds(x_first, nx), pl.ds(ROW0, ny)], local_sem.at[k]) for k in range(2)]
    own.append(pltpu.make_async_copy(disorder_ref, energy.at[pl.ds(x_first, nx), pl.ds(ROW0, ny)], local_sem.at[2]))
    for copy in own:
        copy.start()
    pl.semaphore_wait(barrier, len(SIDES) + 3 * (GROUP - 1))

    buffers = (0, 1, 2, 1, 2)

    def message(e, k, side, part=None):
        dx, dy = SIDES[side]
        width = WIDTHS[e] - (dx != 0 and dy != 0)
        x_from, x_size, x_to = {
            -1: (0, width, x_end),
            0: (0, nx, x_first),
            1: (nx - width, width, x_first - width),
        }[dx]
        y_from, y_size, y_to = {
            -1: (0, width, y_end),
            0: (0, ny, ROW0),
            1: (ny - width, width, ROW0 - width),
        }[dy]
        if part is not None:
            y_from, y_size = ((0, ENDS[e]), (ny - ENDS[e], ENDS[e]), (ENDS[e], ny - 2 * ENDS[e]))[part]
            y_to = ROW0 + y_from
        here = (pl.ds(x_from, x_size), pl.ds(y_from, y_size))
        there = (pl.ds(x_to, x_size), pl.ds(y_to, y_size))
        if k == 2:
            src, dst = disorder_ref.at[here], energy.at[there]
        else:
            b = buffers[e]
            if e == 0:
                src = start_ref.at[(k, *here)]
            else:
                src = v.at[k, b, pl.ds(x_first + x_from, x_size), pl.ds(ROW0 + y_from, y_size)]
            dst = v.at[(k, b, *there)]
        return pltpu.make_async_remote_copy(
            src_ref=src,
            dst_ref=dst,
            send_sem=send_sem.at[e % PARITIES, k],
            recv_sem=recv_sem.at[e % PARITIES, k, 2 if part == 2 else int(side in X_SIDES)],
            device_id=beside(dx, dy),
            device_id_type=MESH,
        )

    def sides_of(e, within=range(len(SIDES))):
        return [side for side in within if WIDTHS[e] > 1 or 0 in SIDES[side]]

    def send(e, k):
        for side in reversed(sides_of(e)):
            if e > 0 and side in X_FACES:
                for part in range(2):
                    message(e, k, side, part).start()
            else:
                message(e, k, side).start()

    def send_middle(e, k):
        for side in X_FACES:
            message(e, k, side, 2).start()

    def rows_of(e, sides):
        total = 0
        for side in sides_of(e, sides):
            dx, dy = SIDES[side]
            width = WIDTHS[e] - (dx != 0 and dy != 0)
            total += (width if dx else nx) * (width if dy else ny)
        return total

    def wait_for(rows, semaphore):
        planes = next(n for n in range(1, v.shape[2]) if rows % n == 0 and rows // n <= v.shape[3])
        whole = v.at[0, 0, pl.ds(0, planes), pl.ds(0, rows // planes)]
        pltpu.make_async_copy(whole, whole, semaphore).wait()

    def middle_rows(e):
        return 2 * WIDTHS[e] * (ny - 2 * ENDS[e]) if e > 0 else 0

    def arrived(e, k, sides):
        rows = rows_of(e, sides) - (middle_rows(e) if sides == X_SIDES else 0)
        wait_for(rows, recv_sem.at[e % PARITIES, k, int(sides == X_SIDES)])

    def middle_arrived(e, k):
        wait_for(middle_rows(e), recv_sem.at[e % PARITIES, k, 2])

    def sent(e, k):
        wait_for(rows_of(e, range(len(SIDES))), send_sem.at[e % PARITIES, k])

    def advance(k, now, before, after, x0, x1, wide, moment=None, between=None):
        r0, r1 = between or ((ROW0 - TILE, y_end + TILE) if wide else (ROW0, y_end))
        factor = (1.0 if before is None else 2.0) / ENERGY_SCALE
        layers, rows = pl.ds(x0, x1 - x0), pl.ds(r0, r1 - r0)
        center = v[k, now, layers, rows, :]
        total = v[k, now, pl.ds(x0 + 1, x1 - x0), rows, :] + v[k, now, pl.ds(x0 - 1, x1 - x0), rows, :]
        total = total + v[k, now, layers, pl.ds(r0 + 1, r1 - r0), :] + v[k, now, layers, pl.ds(r0 - 1, r1 - r0), :]
        total = total + pltpu.roll(center, nz - 1, 2) + pltpu.roll(center, 1, 2)
        result = (energy[layers, rows, :] * center - total) * factor
        if before is not None:
            result = result - v[k, before, layers, rows, :]
        if after is None:
            last_ref[k, pl.ds(x0 - x_first, x1 - x0), pl.ds(r0 - ROW0, r1 - r0)] = result
        else:
            v[k, after, layers, rows, :] = result
        if moment is not None:
            if wide:
                center, result = center[:, TILE:-TILE], result[:, TILE:-TILE]
            of_own = slice(max(x_first - x0, 0), min(x_end, x1) - x0)
            center, result = center[of_own], result[of_own]
            add_moments(k, moment, center, result)

    def add_moments(k, moment, center, result):
        for i, product in enumerate((center * center, center * result)):
            sums[k, 2 * moment + i] += jnp.sum(product.reshape(-1, TILE, nz), axis=0)

    def record(k, now, after, x0, x1, moment):
        at = (pl.ds(x0, x1 - x0), pl.ds(ROW0, ny))
        add_moments(k, moment, v[(k, now, *at)], v[(k, after, *at)])

    def edges(k, now, after, spans_outer, spans_first, spans_next):
        for spans, layers in ((spans_outer, (x_first - 1, x_end)), (spans_first, (x_first, x_end - 1))):
            for x in layers:
                for span in spans:
                    advance(k, now, 0, 0, x, x + 1, False, between=span)
        for x in (x_first, x_end - 2):
            for span in spans_next:
                advance(k, 0, now, after, x, x + 2, False, between=span)

    sums[...] = jnp.zeros_like(sums)
    for k in (0, 2, 1):
        send(0, k)

    for k in range(2):
        own[k].wait()
        if k == 0:
            own[2].wait()
        arrived(0, k, Y_SIDES)
        advance(k, 0, None, 1, x_first + 1, x_end - 1, False, 0)
        arrived(0, k, X_SIDES)
        advance(k, 0, None, 1, x_first, x_first + 1, False, 0)
        advance(k, 0, None, 1, x_end - 1, x_end, False, 0)
        send(1, k)
        send_middle(1, k)

    def sum_message(turn, d):
        return pltpu.make_async_remote_copy(
            src_ref=partial.at[turn, places[turn]],
            dst_ref=partial.at[turn, places[turn]],
            send_sem=sum_send.at[turn],
            recv_sem=sum_recv.at[turn],
            device_id=partner(turn, d),
            device_id_type=MESH,
        )

    def sum_start(turn, row):
        partial[turn, places[turn]] = row
        for d in range(1, GROUP):
            sum_message(turn, d).start()

    def sum_finish(turn):
        others = partial.at[turn, pl.ds(0, GROUP - 1)]
        pltpu.make_async_copy(others, others, sum_recv.at[turn]).wait()
        row = partial[turn, 0]
        for place in range(1, GROUP):
            row = row + partial[turn, place]
        return row

    def own_moments():
        lanes = lax.broadcasted_iota(jnp.int32, (1, nz), 1)
        row = jnp.zeros((1, nz), jnp.float32)
        for k in range(2):
            for i in range(ITERS + 1):
                total = sums[k, i]
                if i >= 2:
                    total = 2.0 * total - sums[k, i % 2]
                total = jnp.sum(total, axis=0, keepdims=True)
                total = jnp.sum(total, axis=1, keepdims=True) / jnp.float32(sites)
                row = row + jnp.where(lanes == k * (nz // 2) + i, total, 0.0)
        return row

    for e in range(1, len(WIDTHS)):
        now, after = buffers[e], (2, 1, 2, None)[e - 1]
        moment, later = ((1, 2), (3, 4), (None, None), (None, None))[e - 1]
        for k in range(2):
            if e == 1 and k == 0:
                arrived(0, 2, Y_SIDES)
            arrived(e, k, Y_SIDES)
            advance(k, now, 0, 0, x_first + 1, x_end - 1, True, moment)
            sent(e - 1, k)
            advance(k, 0, now, after, x_first + 2, x_end - 2, False, later)
            if e == 4 and k == 0:
                sum_start(2, sum_finish(1))
            if e == 1 and k == 0:
                arrived(0, 2, X_SIDES)
            arrived(e, k, X_SIDES)
            low, high = ROW0 + ENDS[e + 1], y_end - ENDS[e + 1]
            ends = ((ROW0, low), (high, y_end))
            edges(k, now, after, ends, ((ROW0 - TILE, low + 1), (high - 1, y_end + TILE)), ends)
            if e + 1 < len(WIDTHS):
                send(e + 1, k)
            if e == 3 and k == 0:
                sum_start(1, sum_finish(0))
            middle_arrived(e, k)
            edges(k, now, after, ((low, high),), ((low + 1, high - 1),), ((low, high),))
            if e + 1 < len(WIDTHS):
                send_middle(e + 1, k)
            if moment is not None:
                for x in (x_first, x_end - 1):
                    record(k, now, 0, x, x + 1, moment)
                for x in (x_first, x_end - 2):
                    record(k, 0, after, x, x + 2, later)
        if e == 2:
            sum_start(0, own_moments())

    row = sum_finish(2)
    moments_ref[0:1, :] = row[:, : ITERS + 1]
    moments_ref[1:2, :] = pltpu.roll(row, nz // 2, 1)[:, : ITERS + 1]
    sent(0, 2)
    for k in range(2):
        sent(len(WIDTHS) - 1, k)
    for turn in range(3):
        others = partial.at[turn, pl.ds(0, GROUP - 1)]
        pltpu.make_async_copy(others, others, sum_send.at[turn]).wait()


def to_hbm(moments_ref, last_ref, moments_out, last_out, sems):
    copies = [pltpu.make_async_copy(moments_ref, moments_out, sems.at[0])]
    copies += [pltpu.make_async_copy(last_ref.at[k], last_out.at[k], sems.at[k + 1]) for k in range(2)]
    for copy in copies:
        copy.start()
    for copy in copies:
        copy.wait()


def local(random_vectors, disorder):
    vectors, nx, ny, nz = random_vectors.shape
    padded = (nx + 2 * HALO, ny + 2 * ROW0, nz)
    outputs = pl.pallas_call(
        body,
        out_shape=(
            pltpu.VMEM((vectors, ITERS + 1), jnp.float32),
            pltpu.VMEM(random_vectors.shape, jnp.float32),
        ),
        in_specs=[pl.BlockSpec(memory_space=pltpu.HBM)] * 2,
        out_specs=(pl.BlockSpec(memory_space=pltpu.VMEM), pl.BlockSpec(memory_space=pltpu.VMEM)),
        scratch_shapes=[
            pltpu.VMEM((vectors, 3, *padded), jnp.float32),
            pltpu.VMEM(padded, jnp.float32),
            pltpu.VMEM((vectors, ITERS + 1, TILE, nz), jnp.float32),
            pltpu.VMEM((3, GROUP, 1, nz), jnp.float32),
            pltpu.SemaphoreType.DMA((3,)),
            pltpu.SemaphoreType.DMA((PARITIES, vectors + 1)),
            pltpu.SemaphoreType.DMA((PARITIES, vectors + 1, 3)),
            pltpu.SemaphoreType.DMA((3,)),
            pltpu.SemaphoreType.DMA((3,)),
        ],
        compiler_params=pltpu.CompilerParams(collective_id=0, has_side_effects=True, vmem_limit_bytes=60 * 2**20),
    )(random_vectors, disorder)
    return pl.pallas_call(
        to_hbm,
        out_shape=(
            jax.ShapeDtypeStruct((vectors, ITERS + 1), jnp.float32),
            jax.ShapeDtypeStruct(random_vectors.shape, jnp.float32),
        ),
        in_specs=[pl.BlockSpec(memory_space=pltpu.VMEM)] * 2,
        out_specs=(pl.BlockSpec(memory_space=pltpu.HBM), pl.BlockSpec(memory_space=pltpu.HBM)),
        scratch_shapes=[pltpu.SemaphoreType.DMA((vectors + 1,))],
        compiler_params=pltpu.CompilerParams(vmem_limit_bytes=2**20),
    )(*outputs)


def solution(mesh):
    placed = (P(None, "gx", "gy", None), P("gx", "gy", None))
    return jax.shard_map(
        local,
        mesh=mesh,
        in_specs=placed,
        out_specs=(P(), P(None, "gx", "gy", None)),
        check_vma=False,
    )
```
